32 devices in a mesh: groups: 2 (over y), owner: 4 (over z), tp: 2 (over x), rep: 2 (over core).
Axes of the slice: x: 2, y: 2, z: 4, core: 2. Of those that a mesh axis runs over, the one named last changes fastest.
Arguments:
- tokens: bfloat16 [2048, 5120], P(('groups', 'owner', 'rep'), 'tp'), parts along dimension 0, may hold values from -6 to 6
- base_projection_weight: bfloat16 [5120, 5120], P('tp', 'owner'), may hold values from -0.078125 to 0.078125
- adapter_down_weight: bfloat16 [32, 5120, 64], P('owner', 'tp'), may hold values from -0.078125 to 0.078125
- adapter_up_weight: bfloat16 [32, 64, 5120], P('owner', None, 'tp'), may hold values from -0.75 to 0.75
- adapter_output_scale: float32 [32], P('owner'), may hold values from 0.5 to 4
- row_owner_index: int32 [2048, 1], P(('groups', 'owner', 'rep')), parts along dimension 0, may hold values from 0 to 3; in each aligned block of 128 rows (0 to 127, 128 to 255, ...) at most 128 rows name the same one
- row_adapter_slot: int32 [2048], P(('groups', 'owner', 'rep')), parts along dimension 0, may hold values from 0 to 7
Outputs:
- projected: bfloat16 [2048, 5120], P(('groups', 'owner', 'rep'), 'tp'), parts along dimension 0
The draws below stay inside these ranges and needn't reach their ends.
There are 2 independent parts, one for each index of `groups`. The reference program is written for one: setup_inputs(seed, part) draws one part's arguments, and reference() takes and returns one part's arrays. A program takes and returns all parts, laid end to end along the dimension named above; an argument that names none is the same for every part. Nothing has to cross between parts.
Inputs may be any that keep to these rules, and one draw needn't show every extreme that they name: `row_owner_index`: among the rows of one device at most 128 name one owner index, and that bound is reached.
All inputs are finite; a program needn't handle non-finite values.
Results may differ from the reference program's by a relative error of at most 0.0056.
Values may be sent and summed in bfloat16 or wider, within the bound.
A program may use at most 128 MiB of HBM per device.

```python
import math
import jax
import jax.numpy as jnp
import numpy as np
from jax import lax

MODEL_WIDTH = 5120
ADAPTER_RANK = 64
ADAPT_DEV = 8
ROW_DEV = 128
ADAPTER_TOTAL = 32
CAP = 128
ROW_TOTAL = 1024


def set_ends(values, stream_key, smallest, high):
    spot = [jax.random.randint(jax.random.fold_in(stream_key, axis), (), 0, length) for axis, length in enumerate(values.shape)]
    widest = values.shape.index(max(values.shape))
    next_to = spot[:widest] + [(spot[widest] + 1) % values.shape[widest]] + spot[widest + 1:]
    return values.at[tuple(spot)].set(smallest).at[tuple(next_to)].set(high)


def steps_of(stream_key, dims, shards, low, top_value):
    gain, own = 1.0, jax.random.fold_in(stream_key, 6)
    for dim, blocks in shards:
        heights = jnp.exp(jax.random.uniform(jax.random.fold_in(own, dim), (blocks,), jnp.float32, low / len(shards), top_value / len(shards)))
        gain = gain * jnp.repeat(heights, dims[dim] // blocks).reshape([-1 if axis == dim else 1 for axis in range(len(dims))])
    return gain


def routed_block(rng, own, number, rows, count, top, most, lean):
    ranking = jax.random.permutation(rng, count)
    heavy_load, ordinary = portions_of(count, rows * top, most, lean, True), portions_of(count, rows * top, most, lean, False)
    places = jnp.arange(count)

    def named(lengths, offset_by):
        used = int((lengths > 0).sum())
        fixed = max(1, used // 4)
        passed = fixed + (places - fixed + offset_by * (used - fixed)) % max(1, count - fixed)
        return jnp.zeros((count,), jnp.int32).at[ranking[jnp.where(places < fixed, places, passed)]].set(jnp.asarray(lengths, jnp.int32))

    lengths = jnp.where(number % 4 == 0, named(heavy_load, number // 4), named(ordinary, number - number // 4 - 1))
    mixed = jax.random.permutation(jax.random.fold_in(own, 3), count)
    donor, receiver = mixed[0:count // 2 * 2:2], mixed[1:count // 2 * 2:2]
    room = jnp.minimum(lengths[donor] - 1, most - lengths[receiver]) // 2
    room = jnp.where((donor == ranking[0]) | (receiver == ranking[0]) | (lengths[receiver] == 0), 0, jnp.maximum(room, 0))
    passed = jax.random.randint(jax.random.fold_in(own, 4), (count // 2,), 0, 1 << 20) % (room + 1)
    lengths = lengths.at[donor].add(-passed).at[receiver].add(passed)
    labels = jnp.searchsorted(jnp.cumsum(lengths), jnp.arange(rows * top), side="right").astype(jnp.int32)
    grid = labels.reshape(top, rows).T
    grid = grid[jax.random.permutation(jax.random.fold_in(own, 1), rows)]
    offset_by = jax.random.randint(jax.random.fold_in(own, 2), (rows, 1), 0, top)
    return jnp.take_along_axis(grid, (jnp.arange(top)[None, :] + offset_by) % top, axis=1)


def portions_of(amount, total, reach, lean, full):
    weights = [(1 << 20) // math.isqrt(rank ** lean) + 1 for rank in range(1, amount + 1)]
    largest = reach if full else min(reach, max(-(-total // amount), total * weights[0] // sum(weights)))
    least = 1 if total - largest >= amount - 1 else 0
    given, surplus = [largest] + [least] * (amount - 1), total - largest - least * (amount - 1)
    while surplus > 0:
        candidates = [i for i in range(1, amount) if given[i] < largest] or [i for i in range(1, amount) if given[i] < reach]
        mass, remaining = sum([weights[i] for i in candidates]), surplus
        for i in candidates:
            addition = min(reach - given[i], max(1, remaining * weights[i] // mass), surplus)
            given[i] = given[i] + addition
            surplus = surplus - addition
    return np.array(given)


def gaussian(stream_key, dims, spread, bound, shards=(), dtype=jnp.bfloat16):
    entries = spread * jax.random.normal(stream_key, dims, jnp.float32)
    if shards:
        entries = entries * steps_of(stream_key, dims, shards, -0.22, 0.18)
    return jnp.clip(entries, -bound, bound).astype(dtype)


def setup_inputs(seed: int = 0, part: int = 0) -> dict:
    key_list = jax.random.split(jax.random.key(seed), 8)
    own_keys = jax.random.split(jax.random.fold_in(key_list[7], part), 8)
    tokens = gaussian(own_keys[0], (ROW_TOTAL, MODEL_WIDTH), 1.0, 6.0, ((0, 8), (1, 2)))
    base_projection_weight = gaussian(key_list[1], (MODEL_WIDTH, MODEL_WIDTH), MODEL_WIDTH ** -0.5, 0.078125, ((0, 2), (1, 4)))
    adapter_down_weight = gaussian(key_list[2], (ADAPTER_TOTAL, MODEL_WIDTH, ADAPTER_RANK), MODEL_WIDTH ** -0.5, 0.078125, ((0, 4), (1, 2)))
    adapter_up_weight = gaussian(key_list[3], (ADAPTER_TOTAL, ADAPTER_RANK, MODEL_WIDTH), ADAPTER_RANK ** -0.5, 0.75, ((0, 4), (2, 2)))
    adapter_output_scale = jnp.clip(jnp.exp(math.log(4.0) - 2.0794415 * jax.random.uniform(key_list[4], (ADAPTER_TOTAL,), jnp.float32) ** steps_of(key_list[4], (ADAPTER_TOTAL,), ((0, 4),), -0.2, 0.2)), 0.5, 4.0)
    row_owner_index_keys = jax.random.split(jax.random.fold_in(own_keys[5], 1), ROW_TOTAL // ROW_DEV)
    row_owner_index_turns = jax.random.permutation(jax.random.fold_in(own_keys[5], 3), ROW_TOTAL // ROW_DEV)
    row_owner_index = jax.vmap(lambda own, number: routed_block(jax.random.fold_in(own_keys[5], 2), own, number, ROW_DEV, ADAPTER_TOTAL // ADAPT_DEV, 1, CAP, 2))(row_owner_index_keys, row_owner_index_turns).reshape((ROW_TOTAL, 1))
    row_adapter_slot = set_ends(jax.random.randint(own_keys[6], (ROW_TOTAL,), 0, ADAPT_DEV), jax.random.fold_in(own_keys[6], 1), 0, ADAPT_DEV - 1).astype(jnp.int32)
    return dict(tokens=tokens, base_projection_weight=base_projection_weight, adapter_down_weight=adapter_down_weight, adapter_up_weight=adapter_up_weight, adapter_output_scale=adapter_output_scale, row_owner_index=row_owner_index, row_adapter_slot=row_adapter_slot)


def reference(tokens, base_projection_weight, adapter_down_weight, adapter_up_weight, adapter_output_scale, row_owner_index, row_adapter_slot):
    base_output = jnp.dot(tokens, base_projection_weight, preferred_element_type=jnp.float32)
    adapter = (row_owner_index[:, 0] * ADAPT_DEV + row_adapter_slot).astype(jnp.int32)
    token_blocks = tokens.reshape(ROW_TOTAL // ROW_DEV, ROW_DEV, MODEL_WIDTH)
    adapter_blocks = adapter.reshape(ROW_TOTAL // ROW_DEV, ROW_DEV)

    def rows_per_block(block_args):
        tok_blk, adapter_block = block_args
        down_weight_rows = adapter_down_weight[adapter_block].astype(jnp.float32)
        low_rank = jnp.einsum("rd,rdk->rk", tok_blk.astype(jnp.float32), down_weight_rows).astype(jnp.bfloat16)
        up_weight_rows = adapter_up_weight[adapter_block].astype(jnp.float32)
        expand = jnp.einsum("rk,rkd->rd", low_rank.astype(jnp.float32), up_weight_rows)
        return (expand * adapter_output_scale[adapter_block][:, None]).astype(jnp.bfloat16)

    adapter_output = lax.map(rows_per_block, (token_blocks, adapter_blocks)).reshape(ROW_TOTAL, MODEL_WIDTH)
    return (base_output + adapter_output.astype(jnp.float32)).astype(jnp.bfloat16)
```

```python
import functools

import jax
import jax.numpy as jnp
from jax import lax
from jax.experimental import pallas as pl
from jax.experimental.pallas import tpu as pltpu
from jax.sharding import PartitionSpec as P


MESH = pl.DeviceIdType.MESH
CHUNKS = 4
TILE = 256


def local(
    tokens,
    base_projection_weight,
    adapter_down_weight,
    adapter_up_weight,
    adapter_output_scale,
    row_owner_index,
    row_adapter_slot,
):
    row_count = tokens.shape[0]
    local_feature_slice = tokens.shape[1]
    owner_devices = lax.axis_size("owner")
    adapter_slots = row_count * 4 // owner_devices
    local_adapter_output = adapter_down_weight.shape[0]
    adapter_rank_width = adapter_down_weight.shape[2]
    gathered, owners_all, slots_all = (
        lax.all_gather(tokens, "owner", axis=0, tiled=True),
        lax.all_gather(row_owner_index, "owner", axis=0, tiled=True),
        lax.all_gather(row_adapter_slot, "owner", axis=0, tiled=True),
    )
    partial_value = jnp.dot(gathered, base_projection_weight, preferred_element_type=jnp.float32)
    partial_value = partial_value.reshape(owner_devices, row_count, base_projection_weight.shape[1])
    returned = lax.all_to_all(partial_value, "owner", split_axis=0, concat_axis=2, tiled=True)
    full_partial = returned.reshape(row_count, owner_devices * base_projection_weight.shape[1])
    base_output = lax.psum_scatter(full_partial, "tp", scatter_dimension=1, tiled=True)
    owner_ids = row_owner_index[:, 0]
    owner_hot = (owner_ids[:, None] == jnp.arange(owner_devices, dtype=jnp.int32)[None, :]).astype(
        jnp.int32
    )
    before = jnp.cumsum(owner_hot, axis=0) - owner_hot
    row_rank = jnp.sum(before * owner_hot, axis=1)
    position = owner_ids * adapter_slots + row_rank
    dispatch = (
        position[None, :] == jnp.arange(owner_devices * adapter_slots, dtype=jnp.int32)[:, None]
    ).astype(jnp.bfloat16)
    my_index = lax.axis_index("owner")
    mine = (owners_all[:, 0] == my_index).astype(jnp.int32).reshape(owner_devices, row_count)
    earlier = jnp.cumsum(mine, axis=1) - mine
    picker = (
        (earlier[:, None, :] == jnp.arange(adapter_slots, dtype=jnp.int32)[None, :, None])
        & (mine[:, None, :] == 1)
    ).astype(jnp.bfloat16)
    arrived_rows = jnp.einsum(
        "scr,srd->scd",
        picker,
        gathered.reshape(owner_devices, row_count, local_feature_slice),
        preferred_element_type=jnp.float32,
    ).astype(jnp.bfloat16)
    codes = (
        jnp.einsum(
            "scr,sr->sc",
            picker,
            (slots_all + 1).astype(jnp.bfloat16).reshape(owner_devices, row_count),
            preferred_element_type=jnp.float32,
        )
        - 1.0
    )
    arrived_codes = codes.astype(jnp.bfloat16)
    items = arrived_rows.shape[1]
    flattened_rows = arrived_rows.reshape(owner_devices * items, local_feature_slice)
    flat_codes = arrived_codes.reshape(owner_devices * items).astype(jnp.float32)
    select = flat_codes[:, None] == jnp.arange(local_adapter_output, dtype=jnp.float32)[None, :]
    select_f = select.astype(jnp.float32)
    gathered_down_output = jnp.einsum(
        "qe,gej->qgj", flattened_rows, adapter_down_weight, preferred_element_type=jnp.float32
    )
    partial_low = jnp.sum(gathered_down_output * select_f[:, :, None], axis=1)
    summed = lax.psum(partial_low, "tp")
    low_rank = summed.astype(jnp.bfloat16)
    spread = (select.astype(jnp.bfloat16)[:, :, None] * low_rank[:, None, :]).reshape(
        owner_devices * items, local_adapter_output * adapter_rank_width
    )
    expand = jnp.dot(
        spread,
        adapter_up_weight.reshape(local_adapter_output * adapter_rank_width, local_feature_slice),
        preferred_element_type=jnp.float32,
    )
    scale_row = jnp.sum(select_f * adapter_output_scale[None, :], axis=1)
    final_output = (
        (expand * scale_row[:, None])
        .astype(jnp.bfloat16)
        .reshape(owner_devices, items, local_feature_slice)
    )
    returned_adapter_output = lax.all_to_all(
        final_output, "owner", split_axis=0, concat_axis=0, tiled=True
    )
    adapter_input_rows = jnp.dot(
        dispatch.T,
        returned_adapter_output.reshape(owner_devices * adapter_slots, local_feature_slice),
        preferred_element_type=jnp.float32,
    )
    return (base_output + adapter_input_rows).astype(jnp.bfloat16)


def chain_kernel(
    slots_per_owner,
    meta_in, scale, tok_hbm, w_hbm, down_hbm, up_hbm, out_ref,
    tok, w, down, up, meta, arrived, result, base_send, base_recv, base_own, low_own, low_recv,
    load_sem, tok_send, tok_recv, res_send, res_recv,
    meta_send, meta_recv, low_ssem, low_rsem, base_ssem, base_rsem,
):
    me = lax.axis_index("owner")
    tp = lax.axis_index("tp")
    rows = tok.shape[1]
    width = w.shape[1]
    features = tok.shape[2]
    chunk = rows // CHUNKS
    low_half = me < 2
    first = (me == 0) | (me == 3)
    second = jnp.logical_not(first)

    def actual(position):
        return jnp.where(low_half, position, 3 - position)

    v0, v1, v2 = actual(0), actual(1), actual(2)
    home = me // (features // width)
    takes_base = tp == home
    column = lax.rem(me, features // width) * width

    def part(c):
        return pl.ds(c * chunk, chunk)

    def remote(src, dst, ssem, rsem, target):
        return pltpu.make_async_remote_copy(
            src_ref=src, dst_ref=dst, send_sem=ssem, recv_sem=rsem,
            device_id={"owner": target}, device_id_type=MESH,
        )

    def across(src, dst, ssem, rsem):
        return pltpu.make_async_remote_copy(
            src_ref=src, dst_ref=dst, send_sem=ssem, recv_sem=rsem,
            device_id={"tp": 1 - tp}, device_id_type=MESH,
        )

    def tok_copy(kind, src, dst_slot, c, target):
        return remote(
            src.at[part(c)], tok.at[dst_slot, part(c)], tok_send.at[kind, c],
            tok_recv.at[dst_slot, c], target,
        )

    def res_copy(slot, dst_slot, c, target):
        return remote(
            result.at[slot, part(c)], arrived.at[dst_slot, part(c)], res_send.at[slot, c],
            res_recv.at[dst_slot, c], target,
        )

    def meta_copy(k):
        return remote(
            meta_in, meta.at[me], meta_send.at[k - 1], meta_recv.at[me], lax.rem(me + k, 4)
        )

    def meta_arrival(k):
        source = lax.rem(me + k, 4)
        return remote(meta_in, meta.at[source], meta_send.at[k - 1], meta_recv.at[source], source)

    def low_copy(slot):
        return across(low_own.at[slot], low_recv.at[slot], low_ssem.at[slot], low_rsem.at[slot])

    def base_copy(slot):
        return across(
            base_send.at[slot], base_recv.at[slot], base_ssem.at[slot], base_rsem.at[slot]
        )

    loads = [
        pltpu.make_async_copy(tok_hbm, tok.at[0], load_sem.at[0]),
        pltpu.make_async_copy(down_hbm, down, load_sem.at[1]),
        pltpu.make_async_copy(w_hbm, w, load_sem.at[2]),
        pltpu.make_async_copy(up_hbm, up, load_sem.at[3]),
    ]
    barrier = pltpu.get_barrier_semaphore()
    for k in range(1, 4):
        pl.semaphore_signal(
            barrier, inc=1, device_id={"owner": lax.rem(me + k, 4)}, device_id_type=MESH
        )
    pl.semaphore_signal(barrier, inc=1, device_id={"tp": 1 - tp}, device_id_type=MESH)
    for load in loads:
        load.start()
    meta[me] = meta_in[...]
    pl.semaphore_wait(barrier, 4)

    for k in range(1, 4):
        meta_copy(k).start()

    @pl.when(first)
    def _():
        for c in range(CHUNKS):
            tok_copy(0, tok_hbm, 1, c, v1).start()

    @pl.when(second)
    def _():
        for c in range(CHUNKS):
            tok_copy(0, tok_hbm, 1, c, v0).start()
            tok_copy(1, tok_hbm, 2, c, v2).start()

    for load in loads:
        load.wait()
    for k in range(1, 4):
        meta_arrival(k).wait_recv()

    lane = lax.broadcasted_iota(jnp.int32, (rows, 128), 1)
    rank = 64
    groups = slots_per_owner * rank // 128

    def codes(slot):
        position = jnp.where(first, slot, jnp.where(slot < 2, 1 - slot, slot))
        line = meta[actual(position)][0:1, :]
        return jnp.broadcast_to(line, (128, rows)).T

    def mask_of(code, j):
        return code == (me * slots_per_owner + (128 // rank) * j + lane // rank).astype(jnp.float32)

    def project(slot):
        code = codes(slot)
        x = tok[slot]
        wide = lax.dot_general(
            x, down[...], (((1,), (1,)), ((), ())), preferred_element_type=jnp.float32
        )
        low = jnp.zeros((rows, 128), jnp.float32)
        for j in range(groups):
            low = low + jnp.where(mask_of(code, j), wide[:, 128 * j:128 * (j + 1)], 0.0)
        low_own[slot] = low
        low_copy(slot).start()

        @pl.loop(0, width // TILE)
        def _(n):
            cols = pl.ds(pl.multiple_of(n * TILE, TILE), TILE)
            value = jnp.dot(tok[slot], w[:, cols], preferred_element_type=jnp.float32)

            @pl.when(takes_base)
            def _():
                base_own[slot, :, cols] = value

            @pl.when(jnp.logical_not(takes_base))
            def _():
                base_send[slot, :, cols] = value.astype(jnp.bfloat16)

        @pl.when(jnp.logical_not(takes_base))
        def _():
            base_copy(slot).start()

    def finish(slot):
        code = codes(slot)
        low_copy(slot).wait_recv()
        low = low_own[slot] + low_recv[slot]
        spread = jnp.concatenate(
            [jnp.where(mask_of(code, j), low, 0.0).astype(jnp.bfloat16) for j in range(groups)],
            axis=1,
        )
        gain = jnp.zeros((rows, 128), jnp.float32)
        for g in range(slots_per_owner):
            mine = code == (me * slots_per_owner + g + 0 * lane).astype(jnp.float32)
            gain = gain + jnp.where(mine, scale[g], 0.0)
        gain = jnp.concatenate([gain] * (TILE // 128), axis=1)

        @pl.loop(0, features // TILE)
        def _(n):
            cols = pl.ds(pl.multiple_of(n * TILE, TILE), TILE)
            value = jnp.dot(spread, up[:, cols], preferred_element_type=jnp.float32)
            result[slot, :, cols] = (value * gain).astype(jnp.bfloat16)

        @pl.when(takes_base)
        def _():
            base_copy(slot).wait_recv()

            @pl.loop(0, width // TILE)
            def _(n):
                here = pl.ds(pl.multiple_of(n * TILE, TILE), TILE)
                there = pl.ds(pl.multiple_of(column + n * TILE, TILE), TILE)
                base = base_own[slot, :, here] + base_recv[slot, :, here].astype(jnp.float32)
                result[slot, :, there] = (
                    result[slot, :, there].astype(jnp.float32) + base
                ).astype(jnp.bfloat16)

    @pl.loop(0, 5)
    def _(step):
        @pl.when(first & (step >= 1) & (step < 4))
        def _():
            for c in range(CHUNKS):
                tok_copy(0, tok_hbm, step, c, v1).wait_recv()

        @pl.when(second & (step == 1))
        def _():
            for c in range(CHUNKS):
                tok_copy(0, tok_hbm, 1, c, v0).wait_recv()
                tok_copy(2, tok.at[1], 3, c, v2).start()
                tok_copy(0, tok_hbm, 2, c, v0).wait_recv()
                tok_copy(3, tok.at[2], 2, c, v0).start()

        @pl.when(second & (step == 3))
        def _():
            for c in range(CHUNKS):
                tok_copy(0, tok_hbm, 3, c, v0).wait_recv()
                tok_copy(4, tok.at[3], 3, c, v0).start()

        @pl.when(step < 4)
        def _():
            project(step)

        done = jnp.where(first, step, step - 1)

        @pl.when((done >= 0) & (done < 4))
        def _():
            finish(done)

        @pl.when(first & (done >= 1) & (done < 4))
        def _():
            for c in range(CHUNKS):
                res_copy(done, done - 1, c, v1).start()

    def add_arrived(slot, source, c):
        res_copy(slot, source, c, v0).wait_recv()
        result[slot, part(c)] = (
            result[slot, part(c)].astype(jnp.float32)
            + arrived[source, part(c)].astype(jnp.float32)
        ).astype(jnp.bfloat16)

    @pl.when(second)
    def _():
        for slot, source, dst, target in ((2, 1, 3, v2), (3, 2, 4, v2), (1, 4, 0, v0)):
            for c in range(CHUNKS):
                add_arrived(slot, source, c)
                res_copy(slot, dst, c, target).start()
        for c in range(CHUNKS):
            add_arrived(0, 3, c)

    for c in range(CHUNKS):
        res_copy(0, 0, c, v0).wait_recv()
        out_ref[part(c)] = (
            result[0, part(c)].astype(jnp.float32) + arrived[0, part(c)].astype(jnp.float32)
        ).astype(jnp.bfloat16)

    for k in range(1, 4):
        meta_copy(k).wait_send()
    for slot in range(4):
        low_copy(slot).wait_send()

    @pl.when(jnp.logical_not(takes_base))
    def _():
        for slot in range(4):
            base_copy(slot).wait_send()

    for c in range(CHUNKS):
        tok_copy(0, tok_hbm, 1, c, v0).wait_send()
        for slot in range(1, 4):
            res_copy(slot, 0, c, v0).wait_send()

    @pl.when(second)
    def _():
        for c in range(CHUNKS):
            for kind in range(1, 5):
                tok_copy(kind, tok_hbm, 1, c, v0).wait_send()


def fused_local(
    tokens,
    base_projection_weight,
    adapter_down_weight,
    adapter_up_weight,
    adapter_output_scale,
    row_owner_index,
    row_adapter_slot,
):
    rows, features = tokens.shape
    width = base_projection_weight.shape[1]
    adapters, _, rank = adapter_down_weight.shape
    deep = adapters * rank
    down = jnp.swapaxes(adapter_down_weight, 1, 2).reshape(deep, features)
    up = adapter_up_weight.reshape(deep, features)
    code = (row_owner_index[:, 0] * adapters + row_adapter_slot).astype(jnp.float32)
    meta = jnp.broadcast_to(code[None, :], (8, rows))
    bf16, f32 = jnp.bfloat16, jnp.float32
    dma = pltpu.SemaphoreType.DMA
    vmem = pl.BlockSpec(memory_space=pltpu.VMEM)
    far = pl.BlockSpec(memory_space=pl.ANY)
    return pl.pallas_call(
        functools.partial(chain_kernel, adapters),
        out_shape=jax.ShapeDtypeStruct((rows, features), bf16),
        in_specs=[vmem, pl.BlockSpec(memory_space=pltpu.SMEM), far, far, far, far],
        out_specs=vmem,
        scratch_shapes=[
            pltpu.VMEM((4, rows, features), bf16),
            pltpu.VMEM((features, width), bf16),
            pltpu.VMEM((deep, features), bf16),
            pltpu.VMEM((deep, features), bf16),
            pltpu.VMEM((4, 8, rows), f32),
            pltpu.VMEM((5, rows, features), bf16),
            pltpu.VMEM((4, rows, features), bf16),
            pltpu.VMEM((4, rows, width), bf16),
            pltpu.VMEM((4, rows, width), bf16),
            pltpu.VMEM((4, rows, width), f32),
            pltpu.VMEM((4, rows, 128), f32),
            pltpu.VMEM((4, rows, 128), f32),
            dma((4,)),
            dma((5, CHUNKS)),
            dma((4, CHUNKS)),
            dma((4, CHUNKS)),
            dma((5, CHUNKS)),
            dma((3,)),
            dma((4,)),
            dma((4,)),
            dma((4,)),
            dma((4,)),
            dma((4,)),
        ],
        compiler_params=pltpu.CompilerParams(
            collective_id=0, has_side_effects=True, vmem_limit_bytes=48 * 2**20
        ),
        cost_estimate=pl.CostEstimate(
            flops=8 * rows * features * (width + 2 * deep),
            bytes_accessed=2 * features * (width + 2 * deep + 2 * rows),
            transcendentals=0,
        ),
    )(meta, adapter_output_scale, tokens, base_projection_weight, down, up)


def fits(mesh):
    return mesh.shape["owner"] == 4 and mesh.shape["tp"] == 2


def solution(mesh):
    return jax.shard_map(
        fused_local if fits(mesh) else local,
        mesh=mesh,
        in_specs=(
            P(("groups", "owner", "rep"), "tp"),
            P("tp", "owner"),
            P("owner", "tp", None),
            P("owner", None, "tp"),
            P("owner"),
            P(("groups", "owner", "rep"), None),
            P(("groups", "owner", "rep")),
        ),
        out_specs=P(("groups", "owner", "rep"), "tp"),
        check_vma=False,
    )
```

```python
import functools

import jax
import jax.numpy as jnp
from jax import lax
from jax.experimental import pallas as pl
from jax.experimental.pallas import tpu as pltpu
from jax.sharding import PartitionSpec as P


MESH = pl.DeviceIdType.MESH
HALVES = 2
CHUNKS = 8
TILE = 256


def local(
    tokens,
    base_projection_weight,
    adapter_down_weight,
    adapter_up_weight,
    adapter_output_scale,
    row_owner_index,
    row_adapter_slot,
):
    row_count = tokens.shape[0]
    local_feature_slice = tokens.shape[1]
    owner_devices = lax.axis_size("owner")
    adapter_slots = row_count * 4 // owner_devices
    local_adapter_output = adapter_down_weight.shape[0]
    adapter_rank_width = adapter_down_weight.shape[2]
    gathered, owners_all, slots_all = (
        lax.all_gather(tokens, "owner", axis=0, tiled=True),
        lax.all_gather(row_owner_index, "owner", axis=0, tiled=True),
        lax.all_gather(row_adapter_slot, "owner", axis=0, tiled=True),
    )
    partial_value = jnp.dot(gathered, base_projection_weight, preferred_element_type=jnp.float32)
    partial_value = partial_value.reshape(owner_devices, row_count, base_projection_weight.shape[1])
    returned = lax.all_to_all(partial_value, "owner", split_axis=0, concat_axis=2, tiled=True)
    full_partial = returned.reshape(row_count, owner_devices * base_projection_weight.shape[1])
    base_output = lax.psum_scatter(full_partial, "tp", scatter_dimension=1, tiled=True)
    owner_ids = row_owner_index[:, 0]
    owner_hot = (owner_ids[:, None] == jnp.arange(owner_devices, dtype=jnp.int32)[None, :]).astype(
        jnp.int32
    )
    before = jnp.cumsum(owner_hot, axis=0) - owner_hot
    row_rank = jnp.sum(before * owner_hot, axis=1)
    position = owner_ids * adapter_slots + row_rank
    dispatch = (
        position[None, :] == jnp.arange(owner_devices * adapter_slots, dtype=jnp.int32)[:, None]
    ).astype(jnp.bfloat16)
    my_index = lax.axis_index("owner")
    mine = (owners_all[:, 0] == my_index).astype(jnp.int32).reshape(owner_devices, row_count)
    earlier = jnp.cumsum(mine, axis=1) - mine
    picker = (
        (earlier[:, None, :] == jnp.arange(adapter_slots, dtype=jnp.int32)[None, :, None])
        & (mine[:, None, :] == 1)
    ).astype(jnp.bfloat16)
    arrived_rows = jnp.einsum(
        "scr,srd->scd",
        picker,
        gathered.reshape(owner_devices, row_count, local_feature_slice),
        preferred_element_type=jnp.float32,
    ).astype(jnp.bfloat16)
    codes = (
        jnp.einsum(
            "scr,sr->sc",
            picker,
            (slots_all + 1).astype(jnp.bfloat16).reshape(owner_devices, row_count),
            preferred_element_type=jnp.float32,
        )
        - 1.0
    )
    arrived_codes = codes.astype(jnp.bfloat16)
    items = arrived_rows.shape[1]
    flattened_rows = arrived_rows.reshape(owner_devices * items, local_feature_slice)
    flat_codes = arrived_codes.reshape(owner_devices * items).astype(jnp.float32)
    select = flat_codes[:, None] == jnp.arange(local_adapter_output, dtype=jnp.float32)[None, :]
    select_f = select.astype(jnp.float32)
    gathered_down_output = jnp.einsum(
        "qe,gej->qgj", flattened_rows, adapter_down_weight, preferred_element_type=jnp.float32
    )
    partial_low = jnp.sum(gathered_down_output * select_f[:, :, None], axis=1)
    summed = lax.psum(partial_low, "tp")
    low_rank = summed.astype(jnp.bfloat16)
    spread = (select.astype(jnp.bfloat16)[:, :, None] * low_rank[:, None, :]).reshape(
        owner_devices * items, local_adapter_output * adapter_rank_width
    )
    expand = jnp.dot(
        spread,
        adapter_up_weight.reshape(local_adapter_output * adapter_rank_width, local_feature_slice),
        preferred_element_type=jnp.float32,
    )
    scale_row = jnp.sum(select_f * adapter_output_scale[None, :], axis=1)
    final_output = (
        (expand * scale_row[:, None])
        .astype(jnp.bfloat16)
        .reshape(owner_devices, items, local_feature_slice)
    )
    returned_adapter_output = lax.all_to_all(
        final_output, "owner", split_axis=0, concat_axis=0, tiled=True
    )
    adapter_input_rows = jnp.dot(
        dispatch.T,
        returned_adapter_output.reshape(owner_devices * adapter_slots, local_feature_slice),
        preferred_element_type=jnp.float32,
    )
    return (base_output + adapter_input_rows).astype(jnp.bfloat16)


def chain_kernel(
    slots_per_owner,
    meta_in, scale, tok_hbm, w_hbm, down_hbm, up_hbm, out_ref,
    tok, w, down, up, meta, arrived, result, base_send, base_recv, base_own, low_own, low_recv, code_of,
    load_sem, tok_send, tok_recv, res_send, res_recv,
    meta_send, meta_recv, low_ssem, low_rsem, base_ssem, base_rsem,
):
    me = lax.axis_index("owner")
    tp = lax.axis_index("tp")
    rows = tok.shape[1]
    width = w.shape[1]
    features = tok.shape[2]
    chunk = rows // CHUNKS
    half = rows // HALVES
    per_half = CHUNKS // HALVES
    low_half = me < 2
    first = (me == 0) | (me == 3)
    second = jnp.logical_not(first)

    def actual(position):
        return jnp.where(low_half, position, 3 - position)

    v0, v1, v2 = actual(0), actual(1), actual(2)
    home = me // (features // width)
    takes_base = tp == home
    column = lax.rem(me, features // width) * width

    def part(c):
        return pl.ds(pl.multiple_of(c * chunk, chunk), chunk)

    def span(h):
        return pl.ds(pl.multiple_of(h * half, half), half)

    def remote(src, dst, ssem, rsem, target):
        return pltpu.make_async_remote_copy(
            src_ref=src, dst_ref=dst, send_sem=ssem, recv_sem=rsem,
            device_id={"owner": target}, device_id_type=MESH,
        )

    def across(src, dst, ssem, rsem):
        return pltpu.make_async_remote_copy(
            src_ref=src, dst_ref=dst, send_sem=ssem, recv_sem=rsem,
            device_id={"tp": 1 - tp}, device_id_type=MESH,
        )

    def tok_copy(kind, src, dst_slot, c, target):
        return remote(
            src.at[span(c)], tok.at[dst_slot, span(c)], tok_send.at[kind, c],
            tok_recv.at[dst_slot, c], target,
        )

    def res_copy(slot, dst_slot, c, target):
        return remote(
            result.at[slot, part(c)], arrived.at[dst_slot, part(c)], res_send.at[slot, c],
            res_recv.at[dst_slot, c], target,
        )

    def meta_copy(k):
        return remote(
            meta_in, meta.at[me], meta_send.at[k - 1], meta_recv.at[me], lax.rem(me + k, 4)
        )

    def meta_arrival(k):
        source = lax.rem(me + k, 4)
        return remote(meta_in, meta.at[source], meta_send.at[k - 1], meta_recv.at[source], source)

    def low_copy(slot, h):
        return across(
            low_own.at[slot, span(h)], low_recv.at[slot, span(h)],
            low_ssem.at[slot, h], low_rsem.at[slot, h],
        )

    def base_copy(slot, h):
        return across(
            base_send.at[slot, span(h)], base_recv.at[slot, span(h)],
            base_ssem.at[slot, h], base_rsem.at[slot, h],
        )

    loads = [
        pltpu.make_async_copy(tok_hbm, tok.at[0], load_sem.at[0]),
        pltpu.make_async_copy(down_hbm, down, load_sem.at[1]),
        pltpu.make_async_copy(w_hbm, w, load_sem.at[2]),
        pltpu.make_async_copy(up_hbm, up, load_sem.at[3]),
    ]
    barrier = pltpu.get_barrier_semaphore()
    for k in range(1, 4):
        pl.semaphore_signal(
            barrier, inc=1, device_id={"owner": lax.rem(me + k, 4)}, device_id_type=MESH
        )
    pl.semaphore_signal(barrier, inc=1, device_id={"tp": 1 - tp}, device_id_type=MESH)
    for load in loads:
        load.start()
    meta[me] = meta_in[...]
    pl.semaphore_wait(barrier, 4)

    for k in range(1, 4):
        meta_copy(k).start()

    @pl.when(first)
    def _():
        for c in range(HALVES):
            tok_copy(0, tok_hbm, 1, c, v1).start()

    @pl.when(second)
    def _():
        for c in range(HALVES):
            tok_copy(0, tok_hbm, 1, c, v0).start()
            tok_copy(1, tok_hbm, 2, c, v2).start()

    for load in loads:
        load.wait()
    for k in range(1, 4):
        meta_arrival(k).wait_recv()

    rank = 64
    groups = slots_per_owner * rank // 128
    for slot in range(4):
        position = jnp.where(first, slot, 1 - slot if slot < 2 else slot)
        line = meta[actual(position)][0:1, :]
        code_of[slot] = jnp.broadcast_to(line, (128, rows)).T
    lane = lax.broadcasted_iota(jnp.int32, (half, 128), 1)

    def mask_of(code, j):
        return code == (me * slots_per_owner + (128 // rank) * j + lane // rank).astype(jnp.float32)

    def project(slot, h):
        here = span(h)
        code = code_of[slot, here]
        wide = lax.dot_general(
            tok[slot, here], down[...], (((1,), (1,)), ((), ())),
            preferred_element_type=jnp.float32,
        )
        low = jnp.zeros((half, 128), jnp.float32)
        for j in range(groups):
            low = low + jnp.where(mask_of(code, j), wide[:, 128 * j:128 * (j + 1)], 0.0)
        low_own[slot, here] = low
        low_copy(slot, h).start()

        @pl.loop(0, width // TILE)
        def _(n):
            cols = pl.ds(pl.multiple_of(n * TILE, TILE), TILE)
            value = jnp.dot(tok[slot, here], w[:, cols], preferred_element_type=jnp.float32)

            @pl.when(takes_base)
            def _():
                base_own[slot, here, cols] = value

            @pl.when(jnp.logical_not(takes_base))
            def _():
                base_send[slot, here, cols] = value.astype(jnp.bfloat16)

        @pl.when(jnp.logical_not(takes_base))
        def _():
            base_copy(slot, h).start()

    def finish(slot, h):
        here = span(h)
        code = code_of[slot, here]
        low_copy(slot, h).wait_recv()
        low = low_own[slot, here] + low_recv[slot, here]
        spread = jnp.concatenate(
            [jnp.where(mask_of(code, j), low, 0.0).astype(jnp.bfloat16) for j in range(groups)],
            axis=1,
        )
        gain = jnp.zeros((half, 128), jnp.float32)
        for g in range(slots_per_owner):
            mine = code == (me * slots_per_owner + g + 0 * lane).astype(jnp.float32)
            gain = gain + jnp.where(mine, scale[g], 0.0)
        gain = jnp.concatenate([gain] * (TILE // 128), axis=1)

        @pl.loop(0, features // TILE)
        def _(n):
            cols = pl.ds(pl.multiple_of(n * TILE, TILE), TILE)
            value = jnp.dot(spread, up[:, cols], preferred_element_type=jnp.float32)
            result[slot, here, cols] = (value * gain).astype(jnp.bfloat16)

        @pl.when(takes_base)
        def _():
            base_copy(slot, h).wait_recv()

            @pl.loop(0, width // TILE)
            def _(n):
                own = pl.ds(pl.multiple_of(n * TILE, TILE), TILE)
                there = pl.ds(pl.multiple_of(column + n * TILE, TILE), TILE)
                base = base_own[slot, here, own] + base_recv[slot, here, own].astype(jnp.float32)
                result[slot, here, there] = (
                    result[slot, here, there].astype(jnp.float32) + base
                ).astype(jnp.bfloat16)

    def item(k):
        slot = jnp.where(k < 2, 0, jnp.where(k < 6, 1 + k % 2, 3))
        h = jnp.where(k < 2, k, jnp.where(k < 6, (k - 2) // 2, k - 6))
        return jnp.where(first, k // HALVES, slot), jnp.where(first, k % HALVES, h)

    total = 4 * HALVES
    lag = jnp.where(first, 0, 2)

    @pl.loop(0, total + 2)
    def _(step):
        now = jnp.minimum(step, total - 1)
        slot, h = item(now)

        @pl.when(first & (step >= HALVES) & (step < total))
        def _():
            tok_copy(0, tok_hbm, slot, h, v1).wait_recv()

        @pl.when(second & ((step == 2) | (step == 4)))
        def _():
            tok_copy(0, tok_hbm, 1, h, v0).wait_recv()
            tok_copy(2, tok.at[1], 3, h, v2).start()
            tok_copy(0, tok_hbm, 2, h, v0).wait_recv()
            tok_copy(3, tok.at[2], 2, h, v0).start()

        @pl.when(second & (step >= 6) & (step < total))
        def _():
            tok_copy(0, tok_hbm, 3, h, v0).wait_recv()
            tok_copy(4, tok.at[3], 3, h, v0).start()

        @pl.when(step < total)
        def _():
            project(slot, h)

        late = jnp.clip(step - lag, 0, total - 1)
        slot_done, h_done = item(late)

        @pl.when((step >= lag) & (step < total + lag))
        def _():
            finish(slot_done, h_done)

        @pl.when(first & (step >= HALVES) & (step < total))
        def _():
            for c in range(per_half):
                res_copy(slot_done, slot_done - 1, h_done * per_half + c, v1).start()

    def add_arrived(slot, source, c):
        res_copy(slot, source, c, v0).wait_recv()
        result[slot, part(c)] = (
            result[slot, part(c)].astype(jnp.float32)
            + arrived[source, part(c)].astype(jnp.float32)
        ).astype(jnp.bfloat16)

    @pl.when(second)
    def _():
        for slot, source, dst, target in ((2, 1, 3, v2), (3, 2, 4, v2), (1, 4, 0, v0)):
            for c in range(CHUNKS):
                add_arrived(slot, source, c)
                res_copy(slot, dst, c, target).start()
        for c in range(CHUNKS):
            add_arrived(0, 3, c)

    for c in range(CHUNKS):
        res_copy(0, 0, c, v0).wait_recv()
        out_ref[part(c)] = (
            result[0, part(c)].astype(jnp.float32) + arrived[0, part(c)].astype(jnp.float32)
        ).astype(jnp.bfloat16)

    for k in range(1, 4):
        meta_copy(k).wait_send()
    for slot in range(4):
        for h in range(HALVES):
            low_copy(slot, h).wait_send()

    @pl.when(jnp.logical_not(takes_base))
    def _():
        for slot in range(4):
            for h in range(HALVES):
                base_copy(slot, h).wait_send()

    for h in range(HALVES):
        tok_copy(0, tok_hbm, 1, h, v0).wait_send()
    for c in range(CHUNKS):
        for slot in range(1, 4):
            res_copy(slot, 0, c, v0).wait_send()

    @pl.when(second)
    def _():
        for h in range(HALVES):
            for kind in range(1, 5):
                tok_copy(kind, tok_hbm, 1, h, v0).wait_send()


def fused_local(
    tokens,
    base_projection_weight,
    adapter_down_weight,
    adapter_up_weight,
    adapter_output_scale,
    row_owner_index,
    row_adapter_slot,
):
    rows, features = tokens.shape
    width = base_projection_weight.shape[1]
    adapters, _, rank = adapter_down_weight.shape
    deep = adapters * rank
    down = jnp.swapaxes(adapter_down_weight, 1, 2).reshape(deep, features)
    up = adapter_up_weight.reshape(deep, features)
    code = (row_owner_index[:, 0] * adapters + row_adapter_slot).astype(jnp.float32)
    meta = jnp.broadcast_to(code[None, :], (8, rows))
    bf16, f32 = jnp.bfloat16, jnp.float32
    dma = pltpu.SemaphoreType.DMA
    vmem = pl.BlockSpec(memory_space=pltpu.VMEM)
    far = pl.BlockSpec(memory_space=pl.ANY)
    return pl.pallas_call(
        functools.partial(chain_kernel, adapters),
        out_shape=jax.ShapeDtypeStruct((rows, features), bf16),
        in_specs=[vmem, pl.BlockSpec(memory_space=pltpu.SMEM), far, far, far, far],
        out_specs=vmem,
        scratch_shapes=[
            pltpu.VMEM((4, rows, features), bf16),
            pltpu.VMEM((features, width), bf16),
            pltpu.VMEM((deep, features), bf16),
            pltpu.VMEM((deep, features), bf16),
            pltpu.VMEM((4, 8, rows), f32),
            pltpu.VMEM((5, rows, features), bf16),
            pltpu.VMEM((4, rows, features), bf16),
            pltpu.VMEM((4, rows, width), bf16),
            pltpu.VMEM((4, rows, width), bf16),
            pltpu.VMEM((4, rows, width), f32),
            pltpu.VMEM((4, rows, 128), f32),
            pltpu.VMEM((4, rows, 128), f32),
            pltpu.VMEM((4, rows, 128), f32),
            dma((4,)),
            dma((5, HALVES)),
            dma((4, HALVES)),
            dma((4, CHUNKS)),
            dma((5, CHUNKS)),
            dma((3,)),
            dma((4,)),
            dma((4, HALVES)),
            dma((4, HALVES)),
            dma((4, HALVES)),
            dma((4, HALVES)),
        ],
        compiler_params=pltpu.CompilerParams(
            collective_id=0, has_side_effects=True, vmem_limit_bytes=62 * 2**20
        ),
        cost_estimate=pl.CostEstimate(
            flops=8 * rows * features * (width + 2 * deep),
            bytes_accessed=2 * features * (width + 2 * deep + 2 * rows),
            transcendentals=0,
        ),
    )(meta, adapter_output_scale, tokens, base_projection_weight, down, up)


def fits(mesh):
    return mesh.shape["owner"] == 4 and mesh.shape["tp"] == 2


def solution(mesh):
    return jax.shard_map(
        fused_local if fits(mesh) else local,
        mesh=mesh,
        in_specs=(
            P(("groups", "owner", "rep"), "tp"),
            P("tp", "owner"),
            P("owner", "tp", None),
            P("owner", None, "tp"),
            P("owner"),
            P(("groups", "owner", "rep"), None),
            P(("groups", "owner", "rep")),
        ),
        out_specs=P(("groups", "owner", "rep"), "tp"),
        check_vma=False,
    )
```

```python
import functools

import jax
import jax.numpy as jnp
from jax import lax
from jax.experimental import pallas as pl
from jax.experimental.pallas import tpu as pltpu
from jax.sharding import PartitionSpec as P


MESH = pl.DeviceIdType.MESH
HALVES = 2
CHUNKS = 4
TILE = 256


def local(
    tokens,
    base_projection_weight,
    adapter_down_weight,
    adapter_up_weight,
    adapter_output_scale,
    row_owner_index,
    row_adapter_slot,
):
    row_count = tokens.shape[0]
    local_feature_slice = tokens.shape[1]
    owner_devices = lax.axis_size("owner")
    adapter_slots = row_count * 4 // owner_devices
    local_adapter_output = adapter_down_weight.shape[0]
    adapter_rank_width = adapter_down_weight.shape[2]
    gathered, owners_all, slots_all = (
        lax.all_gather(tokens, "owner", axis=0, tiled=True),
        lax.all_gather(row_owner_index, "owner", axis=0, tiled=True),
        lax.all_gather(row_adapter_slot, "owner", axis=0, tiled=True),
    )
    partial_value = jnp.dot(gathered, base_projection_weight, preferred_element_type=jnp.float32)
    partial_value = partial_value.reshape(owner_devices, row_count, base_projection_weight.shape[1])
    returned = lax.all_to_all(partial_value, "owner", split_axis=0, concat_axis=2, tiled=True)
    full_partial = returned.reshape(row_count, owner_devices * base_projection_weight.shape[1])
    base_output = lax.psum_scatter(full_partial, "tp", scatter_dimension=1, tiled=True)
    owner_ids = row_owner_index[:, 0]
    owner_hot = (owner_ids[:, None] == jnp.arange(owner_devices, dtype=jnp.int32)[None, :]).astype(
        jnp.int32
    )
    before = jnp.cumsum(owner_hot, axis=0) - owner_hot
    row_rank = jnp.sum(before * owner_hot, axis=1)
    position = owner_ids * adapter_slots + row_rank
    dispatch = (
        position[None, :] == jnp.arange(owner_devices * adapter_slots, dtype=jnp.int32)[:, None]
    ).astype(jnp.bfloat16)
    my_index = lax.axis_index("owner")
    mine = (owners_all[:, 0] == my_index).astype(jnp.int32).reshape(owner_devices, row_count)
    earlier = jnp.cumsum(mine, axis=1) - mine
    picker = (
        (earlier[:, None, :] == jnp.arange(adapter_slots, dtype=jnp.int32)[None, :, None])
        & (mine[:, None, :] == 1)
    ).astype(jnp.bfloat16)
    arrived_rows = jnp.einsum(
        "scr,srd->scd",
        picker,
        gathered.reshape(owner_devices, row_count, local_feature_slice),
        preferred_element_type=jnp.float32,
    ).astype(jnp.bfloat16)
    codes = (
        jnp.einsum(
            "scr,sr->sc",
            picker,
            (slots_all + 1).astype(jnp.bfloat16).reshape(owner_devices, row_count),
            preferred_element_type=jnp.float32,
        )
        - 1.0
    )
    arrived_codes = codes.astype(jnp.bfloat16)
    items = arrived_rows.shape[1]
    flattened_rows = arrived_rows.reshape(owner_devices * items, local_feature_slice)
    flat_codes = arrived_codes.reshape(owner_devices * items).astype(jnp.float32)
    select = flat_codes[:, None] == jnp.arange(local_adapter_output, dtype=jnp.float32)[None, :]
    select_f = select.astype(jnp.float32)
    gathered_down_output = jnp.einsum(
        "qe,gej->qgj", flattened_rows, adapter_down_weight, preferred_element_type=jnp.float32
    )
    partial_low = jnp.sum(gathered_down_output * select_f[:, :, None], axis=1)
    summed = lax.psum(partial_low, "tp")
    low_rank = summed.astype(jnp.bfloat16)
    spread = (select.astype(jnp.bfloat16)[:, :, None] * low_rank[:, None, :]).reshape(
        owner_devices * items, local_adapter_output * adapter_rank_width
    )
    expand = jnp.dot(
        spread,
        adapter_up_weight.reshape(local_adapter_output * adapter_rank_width, local_feature_slice),
        preferred_element_type=jnp.float32,
    )
    scale_row = jnp.sum(select_f * adapter_output_scale[None, :], axis=1)
    final_output = (
        (expand * scale_row[:, None])
        .astype(jnp.bfloat16)
        .reshape(owner_devices, items, local_feature_slice)
    )
    returned_adapter_output = lax.all_to_all(
        final_output, "owner", split_axis=0, concat_axis=0, tiled=True
    )
    adapter_input_rows = jnp.dot(
        dispatch.T,
        returned_adapter_output.reshape(owner_devices * adapter_slots, local_feature_slice),
        preferred_element_type=jnp.float32,
    )
    return (base_output + adapter_input_rows).astype(jnp.bfloat16)


def chain_kernel(
    slots_per_owner,
    meta_in, scale, tok_hbm, w_hbm, down_hbm, up_hbm, out_ref,
    tok, w, down, up, meta, arrived, result, base_send, base_recv, base_own, low_own, low_recv, code_of,
    load_sem, tok_send, tok_recv, res_send, res_recv,
    meta_send, meta_recv, low_ssem, low_rsem, base_ssem, base_rsem,
):
    me = lax.axis_index("owner")
    tp = lax.axis_index("tp")
    rows = tok.shape[1]
    width = w.shape[1]
    features = tok.shape[2]
    chunk = rows // CHUNKS
    half = rows // HALVES
    per_half = CHUNKS // HALVES
    low_half = me < 2
    first = (me == 0) | (me == 3)
    second = jnp.logical_not(first)

    def actual(position):
        return jnp.where(low_half, position, 3 - position)

    v0, v1, v2 = actual(0), actual(1), actual(2)
    home = me // (features // width)
    takes_base = tp == home
    column = lax.rem(me, features // width) * width

    def part(c):
        return pl.ds(pl.multiple_of(c * chunk, chunk), chunk)

    def span(h):
        return pl.ds(pl.multiple_of(h * half, half), half)

    def remote(src, dst, ssem, rsem, target):
        return pltpu.make_async_remote_copy(
            src_ref=src, dst_ref=dst, send_sem=ssem, recv_sem=rsem,
            device_id={"owner": target}, device_id_type=MESH,
        )

    def across(src, dst, ssem, rsem):
        return pltpu.make_async_remote_copy(
            src_ref=src, dst_ref=dst, send_sem=ssem, recv_sem=rsem,
            device_id={"tp": 1 - tp}, device_id_type=MESH,
        )

    def tok_copy(kind, src, dst_slot, c, target):
        return remote(
            src.at[span(c)], tok.at[dst_slot, span(c)], tok_send.at[kind, c],
            tok_recv.at[dst_slot, c], target,
        )

    def res_copy(slot, dst_slot, c, target):
        return remote(
            result.at[slot, part(c)], arrived.at[dst_slot, part(c)], res_send.at[slot, c],
            res_recv.at[dst_slot, c], target,
        )

    def meta_copy(k):
        return remote(
            meta_in, meta.at[me], meta_send.at[k - 1], meta_recv.at[me], lax.rem(me + k, 4)
        )

    def meta_arrival(k):
        source = lax.rem(me + k, 4)
        return remote(meta_in, meta.at[source], meta_send.at[k - 1], meta_recv.at[source], source)

    def low_copy(slot, h):
        return across(
            low_own.at[slot, span(h)], low_recv.at[slot, span(h)],
            low_ssem.at[slot, h], low_rsem.at[slot, h],
        )

    def base_copy(slot, h):
        return across(
            base_send.at[slot, span(h)], base_recv.at[slot, span(h)],
            base_ssem.at[slot, h], base_rsem.at[slot, h],
        )

    loads = [
        pltpu.make_async_copy(tok_hbm, tok.at[0], load_sem.at[0]),
        pltpu.make_async_copy(down_hbm, down, load_sem.at[1]),
        pltpu.make_async_copy(w_hbm, w, load_sem.at[2]),
        pltpu.make_async_copy(up_hbm, up, load_sem.at[3]),
    ]
    barrier = pltpu.get_barrier_semaphore()
    for k in range(1, 4):
        pl.semaphore_signal(
            barrier, inc=1, device_id={"owner": lax.rem(me + k, 4)}, device_id_type=MESH
        )
    pl.semaphore_signal(barrier, inc=1, device_id={"tp": 1 - tp}, device_id_type=MESH)
    for load in loads:
        load.start()
    meta[me] = meta_in[...]
    pl.semaphore_wait(barrier, 4)

    for k in range(1, 4):
        meta_copy(k).start()

    @pl.when(first)
    def _():
        for c in range(HALVES):
            tok_copy(0, tok_hbm, 1, c, v1).start()

    @pl.when(second)
    def _():
        for c in range(HALVES):
            tok_copy(0, tok_hbm, 1, c, v0).start()
            tok_copy(1, tok_hbm, 2, c, v2).start()

    for load in loads:
        load.wait()
    for k in range(1, 4):
        meta_arrival(k).wait_recv()

    rank = 64
    groups = slots_per_owner * rank // 128
    for slot in range(4):
        position = jnp.where(first, slot, 1 - slot if slot < 2 else slot)
        line = meta[actual(position)][0:1, :]
        code_of[slot] = jnp.broadcast_to(line, (128, rows)).T
    lane = lax.broadcasted_iota(jnp.int32, (half, 128), 1)

    def mask_of(code, j):
        return code == (me * slots_per_owner + (128 // rank) * j + lane // rank).astype(jnp.float32)

    def project(slot, h):
        here = span(h)
        code = code_of[slot, here]
        wide = lax.dot_general(
            tok[slot, here], down[...], (((1,), (1,)), ((), ())),
            preferred_element_type=jnp.float32,
        )
        low = jnp.zeros((half, 128), jnp.float32)
        for j in range(groups):
            low = low + jnp.where(mask_of(code, j), wide[:, 128 * j:128 * (j + 1)], 0.0)
        low_own[slot, here] = low
        low_copy(slot, h).start()

        @pl.loop(0, width // TILE)
        def _(n):
            cols = pl.ds(pl.multiple_of(n * TILE, TILE), TILE)
            value = jnp.dot(tok[slot, here], w[:, cols], preferred_element_type=jnp.float32)

            @pl.when(takes_base)
            def _():
                base_own[slot, here, cols] = value

            @pl.when(jnp.logical_not(takes_base))
            def _():
                base_send[slot, here, cols] = value.astype(jnp.bfloat16)

        @pl.when(jnp.logical_not(takes_base))
        def _():
            base_copy(slot, h).start()

    def finish(slot, h):
        here = span(h)
        code = code_of[slot, here]
        low_copy(slot, h).wait_recv()
        low = low_own[slot, here] + low_recv[slot, here]
        spread = jnp.concatenate(
            [jnp.where(mask_of(code, j), low, 0.0).astype(jnp.bfloat16) for j in range(groups)],
            axis=1,
        )
        gain = jnp.zeros((half, 128), jnp.float32)
        for g in range(slots_per_owner):
            mine = code == (me * slots_per_owner + g + 0 * lane).astype(jnp.float32)
            gain = gain + jnp.where(mine, scale[g], 0.0)
        gain = jnp.concatenate([gain] * (TILE // 128), axis=1)

        @pl.loop(0, features // TILE)
        def _(n):
            cols = pl.ds(pl.multiple_of(n * TILE, TILE), TILE)
            value = jnp.dot(spread, up[:, cols], preferred_element_type=jnp.float32)
            result[slot, here, cols] = (value * gain).astype(jnp.bfloat16)

        @pl.when(takes_base)
        def _():
            base_copy(slot, h).wait_recv()

            @pl.loop(0, width // TILE)
            def _(n):
                own = pl.ds(pl.multiple_of(n * TILE, TILE), TILE)
                there = pl.ds(pl.multiple_of(column + n * TILE, TILE), TILE)
                base = base_own[slot, here, own] + base_recv[slot, here, own].astype(jnp.float32)
                result[slot, here, there] = (
                    result[slot, here, there].astype(jnp.float32) + base
                ).astype(jnp.bfloat16)

    def item(k):
        slot = jnp.where(k < 2, 0, jnp.where(k < 6, 1 + k % 2, 3))
        h = jnp.where(k < 2, k, jnp.where(k < 6, (k - 2) // 2, k - 6))
        return jnp.where(first, k // HALVES, slot), jnp.where(first, k % HALVES, h)

    total = 4 * HALVES
    lag = jnp.where(first, 0, 2)

    @pl.loop(0, total + 2)
    def _(step):
        now = jnp.minimum(step, total - 1)
        slot, h = item(now)

        @pl.when(first & (step >= HALVES) & (step < total))
        def _():
            tok_copy(0, tok_hbm, slot, h, v1).wait_recv()

        @pl.when(second & ((step == 2) | (step == 4)))
        def _():
            tok_copy(0, tok_hbm, 1, h, v0).wait_recv()
            tok_copy(2, tok.at[1], 3, h, v2).start()
            tok_copy(0, tok_hbm, 2, h, v0).wait_recv()
            tok_copy(3, tok.at[2], 2, h, v0).start()

        @pl.when(second & (step >= 6) & (step < total))
        def _():
            tok_copy(0, tok_hbm, 3, h, v0).wait_recv()
            tok_copy(4, tok.at[3], 3, h, v0).start()

        @pl.when(step < total)
        def _():
            project(slot, h)

        late = jnp.clip(step - lag, 0, total - 1)
        slot_done, h_done = item(late)

        @pl.when((step >= lag) & (step < total + lag))
        def _():
            finish(slot_done, h_done)

        @pl.when(first & (step >= HALVES) & (step < total))
        def _():
            for c in range(per_half):
                res_copy(slot_done, slot_done - 1, h_done * per_half + c, v1).start()

    def add_arrived(slot, source, c):
        res_copy(slot, source, c, v0).wait_recv()
        result[slot, part(c)] = (
            result[slot, part(c)].astype(jnp.float32)
            + arrived[source, part(c)].astype(jnp.float32)
        ).astype(jnp.bfloat16)

    def pass_on(slot, source, dst, c, target):
        add_arrived(slot, source, c)
        res_copy(slot, dst, c, target).start()

    def deliver(c):
        res_copy(0, 0, c, v0).wait_recv()
        out_ref[part(c)] = (
            result[0, part(c)].astype(jnp.float32) + arrived[0, part(c)].astype(jnp.float32)
        ).astype(jnp.bfloat16)

    @pl.when(second)
    def _():
        for c in range(CHUNKS):
            pass_on(2, 1, 3, c, v2)
        for c in range(CHUNKS + 1):
            if c < CHUNKS:
                pass_on(3, 2, 4, c, v2)
            if c > 0:
                pass_on(1, 4, 0, c - 1, v0)
        for c in range(CHUNKS):
            add_arrived(0, 3, c)
            deliver(c)

    @pl.when(first)
    def _():
        for c in range(CHUNKS):
            deliver(c)

    for k in range(1, 4):
        meta_copy(k).wait_send()
    for slot in range(4):
        for h in range(HALVES):
            low_copy(slot, h).wait_send()

    @pl.when(jnp.logical_not(takes_base))
    def _():
        for slot in range(4):
            for h in range(HALVES):
                base_copy(slot, h).wait_send()

    for h in range(HALVES):
        tok_copy(0, tok_hbm, 1, h, v0).wait_send()
    for c in range(CHUNKS):
        for slot in range(1, 4):
            res_copy(slot, 0, c, v0).wait_send()

    @pl.when(second)
    def _():
        for h in range(HALVES):
            for kind in range(1, 5):
                tok_copy(kind, tok_hbm, 1, h, v0).wait_send()


def fused_local(
    tokens,
    base_projection_weight,
    adapter_down_weight,
    adapter_up_weight,
    adapter_output_scale,
    row_owner_index,
    row_adapter_slot,
):
    rows, features = tokens.shape
    width = base_projection_weight.shape[1]
    adapters, _, rank = adapter_down_weight.shape
    deep = adapters * rank
    down = jnp.swapaxes(adapter_down_weight, 1, 2).reshape(deep, features)
    up = adapter_up_weight.reshape(deep, features)
    code = (row_owner_index[:, 0] * adapters + row_adapter_slot).astype(jnp.float32)
    meta = jnp.broadcast_to(code[None, :], (8, rows))
    bf16, f32 = jnp.bfloat16, jnp.float32
    dma = pltpu.SemaphoreType.DMA
    vmem = pl.BlockSpec(memory_space=pltpu.VMEM)
    far = pl.BlockSpec(memory_space=pl.ANY)
    return pl.pallas_call(
        functools.partial(chain_kernel, adapters),
        out_shape=jax.ShapeDtypeStruct((rows, features), bf16),
        in_specs=[vmem, pl.BlockSpec(memory_space=pltpu.SMEM), far, far, far, far],
        out_specs=vmem,
        scratch_shapes=[
            pltpu.VMEM((4, rows, features), bf16),
            pltpu.VMEM((features, width), bf16),
            pltpu.VMEM((deep, features), bf16),
            pltpu.VMEM((deep, features), bf16),
            pltpu.VMEM((4, 8, rows), f32),
            pltpu.VMEM((5, rows, features), bf16),
            pltpu.VMEM((4, rows, features), bf16),
            pltpu.VMEM((4, rows, width), bf16),
            pltpu.VMEM((4, rows, width), bf16),
            pltpu.VMEM((4, rows, width), f32),
            pltpu.VMEM((4, rows, 128), f32),
            pltpu.VMEM((4, rows, 128), f32),
            pltpu.VMEM((4, rows, 128), f32),
            dma((4,)),
            dma((5, HALVES)),
            dma((4, HALVES)),
            dma((4, CHUNKS)),
            dma((5, CHUNKS)),
            dma((3,)),
            dma((4,)),
            dma((4, HALVES)),
            dma((4, HALVES)),
            dma((4, HALVES)),
            dma((4, HALVES)),
        ],
        compiler_params=pltpu.CompilerParams(
            collective_id=0, has_side_effects=True, vmem_limit_bytes=62 * 2**20
        ),
        cost_estimate=pl.CostEstimate(
            flops=8 * rows * features * (width + 2 * deep),
            bytes_accessed=2 * features * (width + 2 * deep + 2 * rows),
            transcendentals=0,
        ),
    )(meta, adapter_output_scale, tokens, base_projection_weight, down, up)


def fits(mesh):
    return mesh.shape["owner"] == 4 and mesh.shape["tp"] == 2


def solution(mesh):
    return jax.shard_map(
        fused_local if fits(mesh) else local,
        mesh=mesh,
        in_specs=(
            P(("groups", "owner", "rep"), "tp"),
            P("tp", "owner"),
            P("owner", "tp", None),
            P("owner", None, "tp"),
            P("owner"),
            P(("groups", "owner", "rep"), None),
            P(("groups", "owner", "rep")),
        ),
        out_specs=P(("groups", "owner", "rep"), "tp"),
        check_vma=False,
    )
```

```python
import functools

import jax
import jax.numpy as jnp
from jax import lax
from jax.experimental import pallas as pl
from jax.experimental.pallas import tpu as pltpu
from jax.sharding import PartitionSpec as P


MESH = pl.DeviceIdType.MESH
HALVES = 2
CHUNKS = 4
TILE = 256


def local(
    tokens,
    base_projection_weight,
    adapter_down_weight,
    adapter_up_weight,
    adapter_output_scale,
    row_owner_index,
    row_adapter_slot,
):
    row_count = tokens.shape[0]
    local_feature_slice = tokens.shape[1]
    owner_devices = lax.axis_size("owner")
    adapter_slots = row_count * 4 // owner_devices
    local_adapter_output = adapter_down_weight.shape[0]
    adapter_rank_width = adapter_down_weight.shape[2]
    gathered, owners_all, slots_all = (
        lax.all_gather(tokens, "owner", axis=0, tiled=True),
        lax.all_gather(row_owner_index, "owner", axis=0, tiled=True),
        lax.all_gather(row_adapter_slot, "owner", axis=0, tiled=True),
    )
    partial_value = jnp.dot(gathered, base_projection_weight, preferred_element_type=jnp.float32)
    partial_value = partial_value.reshape(owner_devices, row_count, base_projection_weight.shape[1])
    returned = lax.all_to_all(partial_value, "owner", split_axis=0, concat_axis=2, tiled=True)
    full_partial = returned.reshape(row_count, owner_devices * base_projection_weight.shape[1])
    base_output = lax.psum_scatter(full_partial, "tp", scatter_dimension=1, tiled=True)
    owner_ids = row_owner_index[:, 0]
    owner_hot = (owner_ids[:, None] == jnp.arange(owner_devices, dtype=jnp.int32)[None, :]).astype(
        jnp.int32
    )
    before = jnp.cumsum(owner_hot, axis=0) - owner_hot
    row_rank = jnp.sum(before * owner_hot, axis=1)
    position = owner_ids * adapter_slots + row_rank
    dispatch = (
        position[None, :] == jnp.arange(owner_devices * adapter_slots, dtype=jnp.int32)[:, None]
    ).astype(jnp.bfloat16)
    my_index = lax.axis_index("owner")
    mine = (owners_all[:, 0] == my_index).astype(jnp.int32).reshape(owner_devices, row_count)
    earlier = jnp.cumsum(mine, axis=1) - mine
    picker = (
        (earlier[:, None, :] == jnp.arange(adapter_slots, dtype=jnp.int32)[None, :, None])
        & (mine[:, None, :] == 1)
    ).astype(jnp.bfloat16)
    arrived_rows = jnp.einsum(
        "scr,srd->scd",
        picker,
        gathered.reshape(owner_devices, row_count, local_feature_slice),
        preferred_element_type=jnp.float32,
    ).astype(jnp.bfloat16)
    codes = (
        jnp.einsum(
            "scr,sr->sc",
            picker,
            (slots_all + 1).astype(jnp.bfloat16).reshape(owner_devices, row_count),
            preferred_element_type=jnp.float32,
        )
        - 1.0
    )
    arrived_codes = codes.astype(jnp.bfloat16)
    items = arrived_rows.shape[1]
    flattened_rows = arrived_rows.reshape(owner_devices * items, local_feature_slice)
    flat_codes = arrived_codes.reshape(owner_devices * items).astype(jnp.float32)
    select = flat_codes[:, None] == jnp.arange(local_adapter_output, dtype=jnp.float32)[None, :]
    select_f = select.astype(jnp.float32)
    gathered_down_output = jnp.einsum(
        "qe,gej->qgj", flattened_rows, adapter_down_weight, preferred_element_type=jnp.float32
    )
    partial_low = jnp.sum(gathered_down_output * select_f[:, :, None], axis=1)
    summed = lax.psum(partial_low, "tp")
    low_rank = summed.astype(jnp.bfloat16)
    spread = (select.astype(jnp.bfloat16)[:, :, None] * low_rank[:, None, :]).reshape(
        owner_devices * items, local_adapter_output * adapter_rank_width
    )
    expand = jnp.dot(
        spread,
        adapter_up_weight.reshape(local_adapter_output * adapter_rank_width, local_feature_slice),
        preferred_element_type=jnp.float32,
    )
    scale_row = jnp.sum(select_f * adapter_output_scale[None, :], axis=1)
    final_output = (
        (expand * scale_row[:, None])
        .astype(jnp.bfloat16)
        .reshape(owner_devices, items, local_feature_slice)
    )
    returned_adapter_output = lax.all_to_all(
        final_output, "owner", split_axis=0, concat_axis=0, tiled=True
    )
    adapter_input_rows = jnp.dot(
        dispatch.T,
        returned_adapter_output.reshape(owner_devices * adapter_slots, local_feature_slice),
        preferred_element_type=jnp.float32,
    )
    return (base_output + adapter_input_rows).astype(jnp.bfloat16)


def chain_kernel(
    slots_per_owner,
    meta_in, scale, tok_hbm, w_hbm, down_hbm, up_hbm, own_ref, last_ref,
    tok, w, down, up, meta, arrived, result, base_send, base_recv, base_own, low_own, low_recv, code_of,
    load_sem, tok_send, tok_recv, res_send, res_recv,
    meta_send, meta_recv, low_ssem, low_rsem, base_ssem, base_rsem,
):
    me = lax.axis_index("owner")
    tp = lax.axis_index("tp")
    rows = tok.shape[1]
    width = w.shape[1]
    features = tok.shape[2]
    chunk = rows // CHUNKS
    half = rows // HALVES
    per_half = CHUNKS // HALVES
    low_half = me < 2
    first = (me == 0) | (me == 3)
    second = jnp.logical_not(first)

    def actual(position):
        return jnp.where(low_half, position, 3 - position)

    v0, v1, v2 = actual(0), actual(1), actual(2)
    home = me // (features // width)
    takes_base = tp == home
    column = lax.rem(me, features // width) * width

    def part(c):
        return pl.ds(pl.multiple_of(c * chunk, chunk), chunk)

    def span(h):
        return pl.ds(pl.multiple_of(h * half, half), half)

    def remote(src, dst, ssem, rsem, target):
        return pltpu.make_async_remote_copy(
            src_ref=src, dst_ref=dst, send_sem=ssem, recv_sem=rsem,
            device_id={"owner": target}, device_id_type=MESH,
        )

    def across(src, dst, ssem, rsem):
        return pltpu.make_async_remote_copy(
            src_ref=src, dst_ref=dst, send_sem=ssem, recv_sem=rsem,
            device_id={"tp": 1 - tp}, device_id_type=MESH,
        )

    def tok_copy(kind, src, dst_slot, c, target):
        return remote(
            src.at[span(c)], tok.at[dst_slot, span(c)], tok_send.at[kind, c],
            tok_recv.at[dst_slot, c], target,
        )

    def res_copy(slot, dst_slot, c, target):
        return remote(
            result.at[slot, part(c)], arrived.at[dst_slot, part(c)], res_send.at[slot, c],
            res_recv.at[dst_slot, c], target,
        )

    def meta_copy(k):
        return remote(
            meta_in, meta.at[me], meta_send.at[k - 1], meta_recv.at[me], lax.rem(me + k, 4)
        )

    def meta_arrival(k):
        source = lax.rem(me + k, 4)
        return remote(meta_in, meta.at[source], meta_send.at[k - 1], meta_recv.at[source], source)

    def low_copy(slot, h):
        return across(
            low_own.at[slot, span(h)], low_recv.at[slot, span(h)],
            low_ssem.at[slot, h], low_rsem.at[slot, h],
        )

    def base_copy(slot, h):
        return across(
            base_send.at[slot, span(h)], base_recv.at[slot, span(h)],
            base_ssem.at[slot, h], base_rsem.at[slot, h],
        )

    loads = [
        pltpu.make_async_copy(tok_hbm, tok.at[0], load_sem.at[0]),
        pltpu.make_async_copy(down_hbm, down, load_sem.at[1]),
        pltpu.make_async_copy(w_hbm, w, load_sem.at[2]),
        pltpu.make_async_copy(up_hbm, up, load_sem.at[3]),
    ]
    barrier = pltpu.get_barrier_semaphore()
    for k in range(1, 4):
        pl.semaphore_signal(
            barrier, inc=1, device_id={"owner": lax.rem(me + k, 4)}, device_id_type=MESH
        )
    pl.semaphore_signal(barrier, inc=1, device_id={"tp": 1 - tp}, device_id_type=MESH)
    for load in loads:
        load.start()
    meta[me] = meta_in[...]
    pl.semaphore_wait(barrier, 4)

    for k in range(1, 4):
        meta_copy(k).start()

    @pl.when(first)
    def _():
        for c in range(HALVES):
            tok_copy(0, tok_hbm, 1, c, v1).start()

    @pl.when(second)
    def _():
        for c in range(HALVES):
            tok_copy(0, tok_hbm, 1, c, v0).start()
            tok_copy(1, tok_hbm, 2, c, v2).start()

    for load in loads:
        load.wait()
    for k in range(1, 4):
        meta_arrival(k).wait_recv()

    rank = 64
    groups = slots_per_owner * rank // 128
    for slot in range(4):
        position = jnp.where(first, slot, 1 - slot if slot < 2 else slot)
        line = meta[actual(position)][0:1, :]
        code_of[slot] = jnp.broadcast_to(line, (128, rows)).T
    lane = lax.broadcasted_iota(jnp.int32, (half, 128), 1)

    def mask_of(code, j):
        return code == (me * slots_per_owner + (128 // rank) * j + lane // rank).astype(jnp.float32)

    def project(slot, h):
        here = span(h)
        code = code_of[slot, here]
        wide = lax.dot_general(
            tok[slot, here], down[...], (((1,), (1,)), ((), ())),
            preferred_element_type=jnp.float32,
        )
        low = jnp.zeros((half, 128), jnp.float32)
        for j in range(groups):
            low = low + jnp.where(mask_of(code, j), wide[:, 128 * j:128 * (j + 1)], 0.0)
        low_own[slot, here] = low
        low_copy(slot, h).start()

        @pl.loop(0, width // TILE)
        def _(n):
            cols = pl.ds(pl.multiple_of(n * TILE, TILE), TILE)
            value = jnp.dot(tok[slot, here], w[:, cols], preferred_element_type=jnp.float32)

            @pl.when(takes_base)
            def _():
                base_own[slot, here, cols] = value

            @pl.when(jnp.logical_not(takes_base))
            def _():
                base_send[slot, here, cols] = value.astype(jnp.bfloat16)

        @pl.when(jnp.logical_not(takes_base))
        def _():
            base_copy(slot, h).start()

    def finish(slot, h):
        here = span(h)
        code = code_of[slot, here]
        low_copy(slot, h).wait_recv()
        low = low_own[slot, here] + low_recv[slot, here]
        spread = jnp.concatenate(
            [jnp.where(mask_of(code, j), low, 0.0).astype(jnp.bfloat16) for j in range(groups)],
            axis=1,
        )
        gain = jnp.zeros((half, 128), jnp.float32)
        for g in range(slots_per_owner):
            mine = code == (me * slots_per_owner + g + 0 * lane).astype(jnp.float32)
            gain = gain + jnp.where(mine, scale[g], 0.0)
        gain = jnp.concatenate([gain] * (TILE // 128), axis=1)

        @pl.loop(0, features // TILE)
        def _(n):
            cols = pl.ds(pl.multiple_of(n * TILE, TILE), TILE)
            value = jnp.dot(spread, up[:, cols], preferred_element_type=jnp.float32)
            result[slot, here, cols] = (value * gain).astype(jnp.bfloat16)

        @pl.when(takes_base)
        def _():
            base_copy(slot, h).wait_recv()

            @pl.loop(0, width // TILE)
            def _(n):
                own = pl.ds(pl.multiple_of(n * TILE, TILE), TILE)
                there = pl.ds(pl.multiple_of(column + n * TILE, TILE), TILE)
                base = base_own[slot, here, own] + base_recv[slot, here, own].astype(jnp.float32)
                result[slot, here, there] = (
                    result[slot, here, there].astype(jnp.float32) + base
                ).astype(jnp.bfloat16)

    def item(k):
        slot = jnp.where(k < 2, 0, jnp.where(k < 6, 1 + k % 2, 3))
        h = jnp.where(k < 2, k, jnp.where(k < 6, (k - 2) // 2, k - 6))
        return jnp.where(first, k // HALVES, slot), jnp.where(first, k % HALVES, h)

    total = 4 * HALVES
    lag = jnp.where(first, 0, 2)

    @pl.loop(0, total + 2)
    def _(step):
        now = jnp.minimum(step, total - 1)
        slot, h = item(now)

        @pl.when(first & (step >= HALVES) & (step < total))
        def _():
            tok_copy(0, tok_hbm, slot, h, v1).wait_recv()

        @pl.when(second & ((step == 2) | (step == 4)))
        def _():
            tok_copy(0, tok_hbm, 1, h, v0).wait_recv()
            tok_copy(2, tok.at[1], 3, h, v2).start()
            tok_copy(0, tok_hbm, 2, h, v0).wait_recv()
            tok_copy(3, tok.at[2], 2, h, v0).start()

        @pl.when(second & (step >= 6) & (step < total))
        def _():
            tok_copy(0, tok_hbm, 3, h, v0).wait_recv()
            tok_copy(4, tok.at[3], 3, h, v0).start()

        @pl.when(step < total)
        def _():
            project(slot, h)

        late = jnp.clip(step - lag, 0, total - 1)
        slot_done, h_done = item(late)

        @pl.when((step >= lag) & (step < total + lag))
        def _():
            finish(slot_done, h_done)

        @pl.when(first & (step >= HALVES) & (step < total))
        def _():
            for c in range(per_half):
                res_copy(slot_done, slot_done - 1, h_done * per_half + c, v1).start()

    def add_arrived(slot, source, c):
        res_copy(slot, source, c, v0).wait_recv()
        result[slot, part(c)] = (
            result[slot, part(c)].astype(jnp.float32)
            + arrived[source, part(c)].astype(jnp.float32)
        ).astype(jnp.bfloat16)

    def pass_on(slot, source, dst, c, target):
        add_arrived(slot, source, c)
        res_copy(slot, dst, c, target).start()

    def deliver(c):
        res_copy(0, 0, c, v0).wait_recv()
        own_ref[part(c)] = result[0, part(c)]
        last_ref[part(c)] = arrived[0, part(c)]

    @pl.when(second)
    def _():
        for c in range(CHUNKS):
            pass_on(2, 1, 3, c, v2)
        for c in range(CHUNKS + 1):
            if c < CHUNKS:
                pass_on(3, 2, 4, c, v2)
            if c > 0:
                pass_on(1, 4, 0, c - 1, v0)
        for c in range(CHUNKS):
            add_arrived(0, 3, c)
            deliver(c)

    @pl.when(first)
    def _():
        for c in range(CHUNKS):
            deliver(c)

    for k in range(1, 4):
        meta_copy(k).wait_send()
    for slot in range(4):
        for h in range(HALVES):
            low_copy(slot, h).wait_send()

    @pl.when(jnp.logical_not(takes_base))
    def _():
        for slot in range(4):
            for h in range(HALVES):
                base_copy(slot, h).wait_send()

    for h in range(HALVES):
        tok_copy(0, tok_hbm, 1, h, v0).wait_send()
    for c in range(CHUNKS):
        for slot in range(1, 4):
            res_copy(slot, 0, c, v0).wait_send()

    @pl.when(second)
    def _():
        for h in range(HALVES):
            for kind in range(1, 5):
                tok_copy(kind, tok_hbm, 1, h, v0).wait_send()


def fused_local(
    tokens,
    base_projection_weight,
    adapter_down_weight,
    adapter_up_weight,
    adapter_output_scale,
    row_owner_index,
    row_adapter_slot,
):
    rows, features = tokens.shape
    width = base_projection_weight.shape[1]
    adapters, _, rank = adapter_down_weight.shape
    deep = adapters * rank
    down = jnp.swapaxes(adapter_down_weight, 1, 2).reshape(deep, features)
    up = adapter_up_weight.reshape(deep, features)
    code = (row_owner_index[:, 0] * adapters + row_adapter_slot).astype(jnp.float32)
    meta = jnp.broadcast_to(code[None, :], (8, rows))
    bf16, f32 = jnp.bfloat16, jnp.float32
    dma = pltpu.SemaphoreType.DMA
    vmem = pl.BlockSpec(memory_space=pltpu.VMEM)
    far = pl.BlockSpec(memory_space=pl.ANY)
    own, last = pl.pallas_call(
        functools.partial(chain_kernel, adapters),
        out_shape=[jax.ShapeDtypeStruct((rows, features), bf16)] * 2,
        in_specs=[vmem, pl.BlockSpec(memory_space=pltpu.SMEM), far, far, far, far],
        out_specs=[vmem, vmem],
        scratch_shapes=[
            pltpu.VMEM((4, rows, features), bf16),
            pltpu.VMEM((features, width), bf16),
            pltpu.VMEM((deep, features), bf16),
            pltpu.VMEM((deep, features), bf16),
            pltpu.VMEM((4, 8, rows), f32),
            pltpu.VMEM((5, rows, features), bf16),
            pltpu.VMEM((4, rows, features), bf16),
            pltpu.VMEM((4, rows, width), bf16),
            pltpu.VMEM((4, rows, width), bf16),
            pltpu.VMEM((4, rows, width), f32),
            pltpu.VMEM((4, rows, 128), f32),
            pltpu.VMEM((4, rows, 128), f32),
            pltpu.VMEM((4, rows, 128), f32),
            dma((4,)),
            dma((5, HALVES)),
            dma((4, HALVES)),
            dma((4, CHUNKS)),
            dma((5, CHUNKS)),
            dma((3,)),
            dma((4,)),
            dma((4, HALVES)),
            dma((4, HALVES)),
            dma((4, HALVES)),
            dma((4, HALVES)),
        ],
        compiler_params=pltpu.CompilerParams(
            collective_id=0, has_side_effects=True, vmem_limit_bytes=62 * 2**20
        ),
        cost_estimate=pl.CostEstimate(
            flops=8 * rows * features * (width + 2 * deep),
            bytes_accessed=2 * features * (width + 2 * deep + 2 * rows),
            transcendentals=0,
        ),
    )(meta, adapter_output_scale, tokens, base_projection_weight, down, up)
    return (own.astype(f32) + last.astype(f32)).astype(bf16)


def fits(mesh):
    return mesh.shape["owner"] == 4 and mesh.shape["tp"] == 2


def solution(mesh):
    return jax.shard_map(
        fused_local if fits(mesh) else local,
        mesh=mesh,
        in_specs=(
            P(("groups", "owner", "rep"), "tp"),
            P("tp", "owner"),
            P("owner", "tp", None),
            P("owner", None, "tp"),
            P("owner"),
            P(("groups", "owner", "rep"), None),
            P(("groups", "owner", "rep")),
        ),
        out_specs=P(("groups", "owner", "rep"), "tp"),
        check_vma=False,
    )
```
